256 devices in a mesh: layer: 16 (over x, y), row: 2 (over core), col: 8 (over z).
Axes of the slice: x: 4, y: 4, z: 8, core: 2. Of those that a mesh axis runs over, the one named last changes fastest.
Arguments:
- states: bfloat16 [64, 128, 128, 256], P('layer', 'row', 'col'), may hold values from -6 to 6
- weights: bfloat16 [64, 3, 3, 256, 256], P('layer'), may hold values from -0.125 to 0.125
- guess: float32 [16, 128, 128, 256], P('layer', 'row', 'col'), may hold values from -6 to 6
- terminal: float32 [128, 128, 256], P('row', 'col'), may hold values from -6 to 6
Outputs:
- corrected: float32 [16, 128, 128, 256], P('layer', 'row', 'col')
- relaxed: bfloat16 [64, 128, 128, 256], P('layer', 'row', 'col')
The draws below stay inside these ranges and needn't reach their ends.
All inputs are finite; a program needn't handle non-finite values.
Results may differ from the reference program's by a relative error of at most 0.0059.
Values may be sent and summed in bfloat16 or wider, within the bound.
No kernel may reach another device: no remote copies, remote signals or barrier semaphores. Data moves between devices by JAX's collectives and lax.ppermute only.
A program may use at most 128 MiB of HBM per device.

```python
import jax
import jax.numpy as jnp
from jax import lax

C = 256
M = 4
LAYERS = 64
COARSE = 16
HEIGHT = 128
BREADTH = 128


def level_of(rng, extent, shards, least, top_value):
    gain = 1.0
    for dim, shards_of in shards:
        heights = jax.random.uniform(jax.random.fold_in(jax.random.fold_in(rng, 6), dim), (shards_of,), jnp.float32, least / len(shards), top_value / len(shards))
        gain = gain * jnp.repeat(jnp.exp(heights), extent[dim] // shards_of).reshape((-1,) + (1,) * (len(extent) - 1 - dim))
    return gain


def gaussian(stream_key, dims, deviation, reach, cuts=(), kind=jnp.bfloat16):
    array = jax.random.normal(stream_key, dims, jnp.float32) * deviation
    if len(cuts) > 0:
        array = level_of(stream_key, dims, cuts, -0.22, 0.18) * array
    return jnp.clip(array, min=-reach, max=reach).astype(kind)


def setup_inputs(seed: int = 0) -> dict:
    key_of = jax.random.split(jax.random.key(seed), 5)
    states = gaussian(key_of[0], (LAYERS, HEIGHT, BREADTH, C), 1.0, 6.0, ((0, 16), (1, 2), (2, 8)))
    weights = gaussian(key_of[1], (LAYERS, 3, 3, C, C), (9 * C) ** -0.5, 0.125, ((0, 16),))
    guess = gaussian(key_of[2], (COARSE, HEIGHT, BREADTH, C), 1.0, 6.0, ((0, 16), (1, 2), (2, 8)), jnp.float32)
    terminal = gaussian(key_of[3], (HEIGHT, BREADTH, C), 1.0, 6.0, ((0, 2), (1, 8)), jnp.float32)
    return dict(states=states, weights=weights, guess=guess, terminal=terminal)


def conv_adjoint(field, kernel):
    height, breadth, chans = field.shape
    padded = jnp.pad(field.astype(jnp.bfloat16), ((1, 1), (1, 1), (0, 0)))
    total = jnp.zeros((height * breadth, chans), jnp.float32)
    for tap_a in range(3):
        for tap_b in range(3):
            piece = padded[2 - tap_a:2 - tap_a + height, 2 - tap_b:2 - tap_b + breadth].reshape(-1, chans)
            total = total + lax.dot_general(piece, kernel[tap_a, tap_b], (((1,), (1,)), ((), ())), preferred_element_type=jnp.float32)
    return total.reshape(height, breadth, chans)


def adjoint_step(field, forward, kernel, factor):
    gate = (forward > 0).astype(jnp.float32)
    return field + factor * gate * conv_adjoint(field, kernel)


def reference(states, weights, guess, terminal):
    factor = 0.5 / M
    relaxed = []
    residuals = []
    for interval in range(COARSE):
        current = guess[interval + 1] if interval < COARSE - 1 else terminal
        stored = [None] * M
        for inner in range(M - 1, -1, -1):
            layer_id = interval * M + inner
            current = adjoint_step(current, states[layer_id], weights[layer_id], factor)
            stored[inner] = current.astype(jnp.bfloat16)
        relaxed.extend(stored)
        residuals.append(current - guess[interval])
    error = jnp.zeros_like(terminal)
    corrected = [None] * COARSE
    for interval in range(COARSE - 1, -1, -1):
        error = residuals[interval] + adjoint_step(error, states[interval * M], weights[interval * M], M * factor)
        corrected[interval] = guess[interval] + error
    return jnp.stack(corrected), jnp.stack(relaxed)
```

```python
import functools

import jax
import jax.experimental.pallas as pl
import jax.numpy as jnp
from jax import lax
from jax.experimental.pallas import tpu as pltpu
from jax.sharding import PartitionSpec as P

BF = jnp.bfloat16
F32 = jnp.float32
CH = 256
ROWS = 64
PAD = 8
WIN = ROWS + 2 * PAD
COLS = 16
GROUP = 4
DEPTH = 4
STRIP = COLS // GROUP
SEND = STRIP + 2 * (GROUP - 1)
HALO = 7
WIDE = COLS + 2 * HALO
FINE_COLS = (28, 26, 24, 22)
FINE_STEP = (7, 13, 8, 11)
TAPS = 9 * CH


def build(xs, buf, col, x, count):
    size = count * WIN
    below = pltpu.roll(x, size - 1, 0)
    above = pltpu.roll(x, 1, 0)
    for tap, value in enumerate((below, x, above)):
        xs[buf, pl.ds(col, count), :, tap * CH : (tap + 1) * CH] = value.astype(BF).reshape(count, WIN, CH)


def conv(xs, buf, col, count, w_ref, slot):
    total = None
    for b in range(3):
        for a in range(3):
            piece = xs[buf, pl.ds(col + 2 - b, count), :, a * CH : (a + 1) * CH].reshape(count * WIN, CH)
            tap = (a * 3 + b) * CH
            part = lax.dot_general(
                piece, w_ref[slot, tap : tap + CH, :], (((1,), (1,)), ((), ())), preferred_element_type=F32
            )
            total = part if total is None else total + part
    return total


def place(cur, col, count, rows_ref, piece, core):
    cur[col : col + count, PAD : PAD + ROWS, :] = piece.astype(F32)
    other = rows_ref[col : col + count].astype(F32)
    cur[col : col + count, 0:PAD, :] = jnp.where(core == 1, other, 0.0)
    cur[col : col + count, PAD + ROWS : WIN, :] = jnp.where(core == 0, other, 0.0)


def fine_kernel(core_ref, mid_ref, left_ref, right_ref, rows_ref, side_hbm, w_hbm, relaxed_ref, r_ref,
                cur, xs, coarse, side, w, side_sem, w_sem):
    offsets = (0, 28, 54, 78)
    side_copies = [
        pltpu.make_async_copy(side_hbm.at[pl.ds(o, n)], side.at[pl.ds(o, n)], side_sem.at[i])
        for i, (o, n) in enumerate(zip(offsets, FINE_COLS))
    ]
    w_copies = [pltpu.make_async_copy(w_hbm.at[i], w.at[i], w_sem.at[i]) for i in range(DEPTH)]
    for step in (3, 0, 1, 2):
        w_copies[DEPTH - 1 - step].start()
        side_copies[step].start()
    core = core_ref[0]
    place(cur, 0, HALO, rows_ref, left_ref[...], core)
    place(cur, HALO, COLS, rows_ref, mid_ref[...], core)
    place(cur, HALO + COLS, HALO, rows_ref, right_ref[...], core)

    @pl.loop(0, WIDE // 5)
    def _(t):
        build(xs, 0, t * 5, cur[pl.ds(t * 5, 5)].reshape(5 * WIN, CH), 5)

    w_copies[0].wait()
    side_copies[3].wait()

    @pl.loop(0, 2)
    def _(t):
        col = t * 11
        gate = side[pl.ds(offsets[3] + col, 11)].reshape(11 * WIN, CH) > 0
        change = conv(xs, 0, col + 3, 11, w, 0)
        x = cur[pl.ds(col + 4, 11)].reshape(11 * WIN, CH) + jnp.where(gate, 0.5 * change, 0.0)
        coarse[pl.ds(col, 11)] = x.reshape(11, WIN, CH)

    for step in range(DEPTH):
        layer = DEPTH - 1 - step
        if step < DEPTH - 1:
            w_copies[layer].wait()
            side_copies[step].wait()
        count = FINE_STEP[step]
        source = step % 2

        @pl.loop(0, FINE_COLS[step] // count)
        def _(t):
            col = t * count
            gate = side[pl.ds(offsets[step] + col, count)].reshape(count * WIN, CH) > 0
            change = conv(xs, source, col, count, w, layer)
            x = cur[pl.ds(col + 1, count)].reshape(count * WIN, CH) + jnp.where(gate, 0.125 * change, 0.0)
            cur[pl.ds(col, count)] = x.reshape(count, WIN, CH)
            if step < DEPTH - 1:
                build(xs, 1 - source, col, x, count)
            else:
                r_ref[pl.ds(col, count)] = (x.reshape(count, WIN, CH) - coarse[pl.ds(col, count)]).astype(BF)

        first = HALO - 1 - step
        relaxed_ref[layer] = cur[first : first + COLS, PAD : PAD + ROWS, :].astype(BF)


def fine_call(core, mid, left, right, rows, side, w):
    vmem = pl.BlockSpec(memory_space=pltpu.VMEM)
    hbm = pl.BlockSpec(memory_space=pl.ANY)
    return pl.pallas_call(
        fine_kernel,
        out_shape=(
            jax.ShapeDtypeStruct((DEPTH, COLS, ROWS, CH), BF),
            jax.ShapeDtypeStruct((22, WIN, CH), BF),
        ),
        in_specs=[pl.BlockSpec(memory_space=pltpu.SMEM), vmem, vmem, vmem, vmem, hbm, hbm],
        out_specs=(vmem, vmem),
        scratch_shapes=[
            pltpu.VMEM((WIDE, WIN, CH), F32),
            pltpu.VMEM((2, WIDE, WIN, 3 * CH), BF),
            pltpu.VMEM((22, WIN, CH), F32),
            pltpu.VMEM((100, WIN, CH), BF),
            pltpu.VMEM((DEPTH, TAPS, CH), BF),
            pltpu.SemaphoreType.DMA((DEPTH,)),
            pltpu.SemaphoreType.DMA((DEPTH,)),
        ],
        compiler_params=pltpu.CompilerParams(vmem_limit_bytes=48 * 2**20),
        cost_estimate=pl.CostEstimate(flops=2 * 9760 * TAPS * CH, bytes_accessed=14 * 2**20, transcendentals=0),
    )(core, mid, left, right, rows, side, w)


def turn_kernel(first, *refs):
    (place_ref, term_ref), refs = refs[:2], refs[2:]
    if not first:
        (mid_ref, left_ref, right_ref, rows_ref), refs = refs[:4], refs[4:]
    r_hbm, gate_hbm, half_hbm, other_hbm = refs[0:4], refs[4:8], refs[8:12], refs[12:16]
    out_ref, cur, xs, r, gate, w, r_sem, gate_sem, half_sem, other_sem = refs[16:]
    core, spot = place_ref[0], place_ref[1]
    near = pl.multiple_of(core * (TAPS // 2), 16)
    far = pl.multiple_of((1 - core) * (TAPS // 2), 16)

    def copies(slot):
        return (
            [pltpu.make_async_copy(r_hbm[k], r.at[slot(k)], r_sem.at[slot(k)]) for k in range(GROUP)],
            [pltpu.make_async_copy(gate_hbm[k], gate.at[slot(k)], gate_sem.at[slot(k)]) for k in range(GROUP)],
            [pltpu.make_async_copy(half_hbm[k], w.at[slot(k), pl.ds(near, TAPS // 2)], half_sem.at[slot(k)]) for k in range(GROUP)],
            [pltpu.make_async_copy(other_hbm[k], w.at[slot(k), pl.ds(far, TAPS // 2)], other_sem.at[slot(k)]) for k in range(GROUP)],
        )

    started = copies(lambda k: lax.rem(spot + GROUP - k, GROUP))
    for k in range(GROUP):
        for kind in started:
            kind[k].start()
    waits = copies(lambda k: k)

    if first:
        cur[...] = term_ref[...].astype(F32)
    else:
        top = place_ref[2] == 1

        @pl.when(top)
        def _():
            cur[...] = term_ref[...].astype(F32)

        @pl.when(jnp.logical_not(top))
        def _():
            place(cur, 0, STRIP, rows_ref, left_ref[...], core)
            place(cur, STRIP, STRIP, rows_ref, mid_ref[...], core)
            place(cur, 2 * STRIP, STRIP, rows_ref, right_ref[...], core)

    for col in (0, 6):
        build(xs, 0, col, cur[col : col + 6].reshape(6 * WIN, CH), 6)

    for step in range(GROUP):
        layer = GROUP - 1 - step
        count = SEND - 2 * step
        source = step % 2
        waits[0][layer].wait()
        waits[1][layer].wait()
        waits[2][layer].wait()
        waits[3][layer].wait()
        x = r[layer, step : step + count].reshape(count * WIN, CH).astype(F32)
        open_ = gate[layer, step : step + count].reshape(count * WIN, CH) > 0
        change = conv(xs, source, 0, count, w, layer)
        x = x + (cur[1 : 1 + count].reshape(count * WIN, CH) + jnp.where(open_, 0.5 * change, 0.0))
        field = x.reshape(count, WIN, CH)
        if step < GROUP - 1:
            cur[0:count] = field
            build(xs, 1 - source, 0, x, count)
        inner = GROUP - 1 - step
        out_ref[layer] = field[inner : inner + STRIP, PAD : PAD + ROWS, :].astype(BF)


def turn_call(place_info, term, incoming, r, gate, half, other):
    first = incoming is None
    vmem = pl.BlockSpec(memory_space=pltpu.VMEM)
    hbm = pl.BlockSpec(memory_space=pl.ANY)
    pieces = () if first else incoming
    return pl.pallas_call(
        functools.partial(turn_kernel, first),
        out_shape=jax.ShapeDtypeStruct((GROUP, STRIP, ROWS, CH), BF),
        in_specs=[pl.BlockSpec(memory_space=pltpu.SMEM), vmem] + [vmem] * len(pieces) + [hbm] * 16,
        out_specs=vmem,
        scratch_shapes=[
            pltpu.VMEM((3 * STRIP, WIN, CH), F32),
            pltpu.VMEM((2, 3 * STRIP, WIN, 3 * CH), BF),
            pltpu.VMEM((GROUP, SEND, WIN, CH), BF),
            pltpu.VMEM((GROUP, SEND, WIN, CH), BF),
            pltpu.VMEM((GROUP, TAPS, CH), BF),
        ]
        + [pltpu.SemaphoreType.DMA((GROUP,))] * 4,
        compiler_params=pltpu.CompilerParams(vmem_limit_bytes=48 * 2**20),
        cost_estimate=pl.CostEstimate(flops=2 * 2240 * TAPS * CH, bytes_accessed=8 * 2**20, transcendentals=0),
    )(place_info, term, *pieces, *r, *gate, *half, *other)


def on_device(states, weights, guess, terminal):
    position = lax.axis_index("layer")
    core = lax.axis_index("row")
    count = lax.axis_size("layer")
    zs = lax.axis_size("col")
    spot = lax.rem(position, GROUP)

    def layer_perm(value, shift_in_group):
        pairs = [(d, d // GROUP * GROUP + (d + shift_in_group) % GROUP) for d in range(count)]
        return lax.ppermute(value, "layer", pairs)

    def z_up(value):
        return lax.ppermute(value, "col", [(i, i + 1) for i in range(zs - 1)])

    def z_down(value):
        return lax.ppermute(value, "col", [(i + 1, i) for i in range(zs - 1)])

    def core_swap(value):
        return lax.ppermute(value, "row", [(0, 1), (1, 0)])

    def edge_rows(value):
        return jnp.where(core == 0, value[..., ROWS - PAD :, :], value[..., :PAD, :])

    own = jnp.transpose(guess[0].astype(BF), (1, 0, 2))
    above = lax.ppermute(own, "layer", [(d, d - 1) for d in range(1, count)])

    turned = jnp.transpose(states, (0, 2, 1, 3))
    term = jnp.transpose(terminal.astype(BF), (1, 0, 2))
    fields = [(turned[3], 6), (turned[2], 5), (turned[1], 4), (turned[0], 3), (term, STRIP)]
    lasts = z_up(jnp.concatenate([f[COLS - h :] for f, h in fields], axis=0))
    leads = z_down(jnp.concatenate([f[:h] for f, h in fields], axis=0))
    parts, at = [], 0
    for f, h in fields:
        parts += [lasts[at : at + h], f, leads[at : at + h]]
        at += h
    side = jnp.concatenate(parts, axis=0)
    edge = core_swap(edge_rows(side))
    none = jnp.zeros_like(edge)
    side = jnp.concatenate([jnp.where(core == 1, edge, none), side, jnp.where(core == 0, edge, none)], axis=1)

    def strip(window, target, size=SEND):
        return lax.dynamic_slice_in_dim(window, target * STRIP, size, axis=0)

    gate_window = side[78:100]
    flat = weights.reshape(DEPTH, TAPS, CH)
    half = lax.dynamic_slice_in_dim(flat[0], core * (TAPS // 2), TAPS // 2, axis=0)
    rest = lax.dynamic_slice_in_dim(flat[0], (1 - core) * (TAPS // 2), TAPS // 2, axis=0)
    halves = [half] + [layer_perm(half, k) for k in range(1, GROUP)]
    gates = [strip(gate_window, spot)] + [
        layer_perm(strip(gate_window, lax.rem(spot + k, GROUP)), k) for k in range(1, GROUP)
    ]
    others = [rest] + [core_swap(h) for h in halves[1:]]

    mid = jnp.where(position == count - 1, term, above)
    left = z_up(mid[COLS - HALO :])
    right = z_down(mid[:HALO])
    rows = core_swap(jnp.concatenate([edge_rows(left), edge_rows(mid), edge_rows(right)], axis=0))
    core_info = jnp.reshape(core, (1,)).astype(jnp.int32)
    relaxed, r_window = fine_call(core_info, mid, left, right, rows, side, flat)
    relaxed = jnp.transpose(relaxed, (0, 2, 1, 3))

    rs = [strip(r_window, spot)] + [
        layer_perm(strip(r_window, lax.rem(spot + k, GROUP)), k) for k in range(1, GROUP)
    ]

    groups = count // GROUP
    top = (position >= count - GROUP).astype(jnp.int32)
    place_info = jnp.stack([core, spot, top]).astype(jnp.int32)
    term_strip = strip(side[100:], spot, 3 * STRIP)
    tiles = GROUP * zs

    def across(value, shift):
        pairs = []
        for x in range(1, groups):
            for tile in range(tiles):
                target = tile + shift
                if 0 <= target < tiles:
                    start = (x * GROUP + tile % GROUP) * zs + tile // GROUP
                    end = ((x - 1) * GROUP + target % GROUP) * zs + target // GROUP
                    pairs.append((start, end))
        return lax.ppermute(value, ("layer", "col"), pairs)

    fields = turn_call(place_info, term_strip, None, rs, gates, halves, others)
    for _ in range(groups - 1):
        lowest = fields[0]
        e_mid, e_left, e_right = across(lowest, 0), across(lowest, 1), across(lowest, -1)
        e_rows = core_swap(jnp.concatenate([edge_rows(e_left), edge_rows(e_mid), edge_rows(e_right)], axis=0))
        fields = turn_call(place_info, term_strip, (e_mid, e_left, e_right, e_rows), rs, gates, halves, others)

    back = [lax.dynamic_index_in_dim(fields, spot, 0, keepdims=False)] + [
        layer_perm(lax.dynamic_index_in_dim(fields, lax.rem(spot + k, GROUP), 0, keepdims=False), k)
        for k in range(1, GROUP)
    ]
    stacked = jnp.stack(back)
    ordered = jnp.concatenate(
        [
            lax.dynamic_index_in_dim(stacked, lax.rem(spot + GROUP - s, GROUP), 0, keepdims=False)
            for s in range(GROUP)
        ],
        axis=0,
    )
    corrected = ordered.astype(F32)
    return (jnp.transpose(corrected, (1, 0, 2))[None], relaxed)


def solution(mesh):
    in_specs = (
        P("layer", "row", "col", None),
        P("layer", None, None, None, None),
        P("layer", "row", "col", None),
        P("row", "col", None),
    )
    out_specs = (P("layer", "row", "col", None), P("layer", "row", "col", None))
    return jax.shard_map(on_device, mesh=mesh, in_specs=in_specs, out_specs=out_specs, check_vma=False)
```

```python
import functools

import jax
import jax.experimental.pallas as pl
import jax.numpy as jnp
from jax import lax
from jax.experimental.pallas import tpu as pltpu
from jax.sharding import Mesh
from jax.sharding import PartitionSpec as P

BF = jnp.bfloat16
F32 = jnp.float32
CH = 256
ROWS = 64
PAD = 8
WIN = ROWS + 2 * PAD
COLS = 16
GROUP = 4
DEPTH = 4
STRIP = COLS // GROUP
SEND = STRIP + 2 * (GROUP - 1)
HALO = 7
WIDE = COLS + 2 * HALO
FINE_COLS = (28, 26, 24, 22)
HALF = 9 * CH // 2
CHUNK = 5
FINE_VMEM = 24 * 2**20
TURN_VMEM = 10 * 2**20
TAPS = 9 * CH


def build(xs, buf, col, x, count):
    field = x.reshape(count, WIN, CH)
    below = pltpu.roll(field, WIN - 1, 1)
    above = pltpu.roll(field, 1, 1)
    for tap, value in enumerate((below, field, above)):
        xs[buf, pl.ds(col, count), :, tap * CH : (tap + 1) * CH] = value.astype(BF)


def conv(xs, buf, col, count, w_ref, slot):
    total = None
    for b in range(3):
        for a in range(3):
            piece = xs[buf, pl.ds(col + 2 - b, count), :, a * CH : (a + 1) * CH].reshape(count * WIN, CH)
            tap = (a * 3 + b) * CH
            part = lax.dot_general(
                piece, w_ref[slot, tap : tap + CH, :], (((1,), (1,)), ((), ())), preferred_element_type=F32
            )
            total = part if total is None else total + part
    return total


def place(cur, col, count, piece, block):
    cur[col : col + count, 0:ROWS, :] = piece.astype(F32)
    cur[col : col + count, ROWS:WIN, :] = block.astype(F32)


def in_chunks(total, body):
    for col in range(0, total, CHUNK):
        body(col, min(CHUNK, total - col))


FIELDS = ((0, 6), (6, 5), (11, 4), (15, 3))
STARTS = (0, 28, 54, 78)


def fine_kernel(info_ref, mid_ref, left_ref, right_ref, rows_ref, own_hbm, lasts_hbm, leads_hbm, edge_hbm, outer_hbm, w,
                relaxed_ref, r0_ref, r1_ref, r2_ref, r3_ref, cur, xs, coarse, window, side, side_sem):
    side_copies = []
    for step in range(DEPTH):
        at, halo = FIELDS[step]
        start = STARTS[step]
        layer = DEPTH - 1 - step
        moves = (
            (lasts_hbm.at[pl.ds(at, halo)], side.at[pl.ds(start, halo), pl.ds(0, ROWS)]),
            (own_hbm.at[layer], side.at[pl.ds(start + halo, COLS), pl.ds(0, ROWS)]),
            (leads_hbm.at[pl.ds(at, halo)], side.at[pl.ds(start + halo + COLS, halo), pl.ds(0, ROWS)]),
            (outer_hbm.at[pl.ds(at, halo)], side.at[pl.ds(start, halo), pl.ds(ROWS, 2 * PAD)]),
            (edge_hbm.at[layer], side.at[pl.ds(start + halo, COLS), pl.ds(ROWS, 2 * PAD)]),
            (outer_hbm.at[pl.ds(18 + at, halo)], side.at[pl.ds(start + halo + COLS, halo), pl.ds(ROWS, 2 * PAD)]),
        )
        side_copies.append([pltpu.make_async_copy(a, b, side_sem.at[step, i]) for i, (a, b) in enumerate(moves)])
    for step in (3, 0, 1, 2):
        for copy in side_copies[step]:
            copy.start()
    spot = info_ref[1]
    place(cur, 0, HALO, left_ref[...], rows_ref[0:HALO])
    place(cur, HALO, COLS, mid_ref[...], rows_ref[HALO : HALO + COLS])
    place(cur, HALO + COLS, HALO, right_ref[...], rows_ref[HALO + COLS : WIDE])
    in_chunks(WIDE, lambda col, count: build(xs, 0, col, cur[col : col + count], count))

    def wait(step):
        for copy in side_copies[step]:
            copy.wait()

    wait(3)

    def coarse_chunk(col, count):
        gate = side[pl.ds(STARTS[3] + col, count)].reshape(count * WIN, CH) > 0
        change = conv(xs, 0, col + 3, count, w, 0)
        x = cur[pl.ds(col + 4, count)].reshape(count * WIN, CH) + jnp.where(gate, 0.5 * change, 0.0)
        coarse[pl.ds(col, count)] = x.reshape(count, WIN, CH)

    in_chunks(22, coarse_chunk)

    for step in range(DEPTH):
        layer = DEPTH - 1 - step
        if step < DEPTH - 1:
            wait(step)

        def chunk(col, count):
            gate = side[pl.ds(STARTS[step] + col, count)].reshape(count * WIN, CH) > 0
            change = conv(xs, step % 2, col, count, w, layer)
            x = cur[pl.ds(col + 1, count)].reshape(count * WIN, CH) + jnp.where(gate, 0.125 * change, 0.0)
            field = x.reshape(count, WIN, CH)
            cur[pl.ds(col, count)] = field
            if step < DEPTH - 1:
                build(xs, 1 - step % 2, col, field, count)
            else:
                window[pl.ds(col, count)] = (field - coarse[pl.ds(col, count)]).astype(BF)

        in_chunks(FINE_COLS[step], chunk)
        first = HALO - 1 - step
        relaxed_ref[layer] = cur[first : first + COLS, 0:ROWS, :].astype(BF)
    for k, ref in enumerate((r0_ref, r1_ref, r2_ref, r3_ref)):
        ref[...] = window[pl.ds(lax.rem(spot + k, GROUP) * STRIP, SEND)]


def fine_call(info, mid, left, right, rows, own, lasts, leads, edge, outer, w):
    vmem = pl.BlockSpec(memory_space=pltpu.VMEM)
    hbm = pl.BlockSpec(memory_space=pl.ANY)
    return pl.pallas_call(
        fine_kernel,
        out_shape=(jax.ShapeDtypeStruct((DEPTH, COLS, ROWS, CH), BF),)
        + (jax.ShapeDtypeStruct((SEND, WIN, CH), BF),) * GROUP,
        in_specs=[pl.BlockSpec(memory_space=pltpu.SMEM)] + [vmem] * 4 + [hbm] * 5 + [vmem],
        out_specs=(vmem,) * (1 + GROUP),
        scratch_shapes=[
            pltpu.VMEM((WIDE, WIN, CH), F32),
            pltpu.VMEM((2, WIDE, WIN, 3 * CH), BF),
            pltpu.VMEM((22, WIN, CH), F32),
            pltpu.VMEM((22, WIN, CH), BF),
            pltpu.VMEM((100, WIN, CH), BF),
            pltpu.SemaphoreType.DMA((DEPTH, 6)),
        ],
        compiler_params=pltpu.CompilerParams(vmem_limit_bytes=FINE_VMEM),
        cost_estimate=pl.CostEstimate(flops=2 * 9760 * TAPS * CH, bytes_accessed=14 * 2**20, transcendentals=0),
    )(info, mid, left, right, rows, own, lasts, leads, edge, outer, w)


def gate_kernel(info_ref, own0, own1, own2, own3, term_own, lasts, leads, edge, h0, h1, h2, h3, o0, o1, o2, o3,
                gate_ref, term_ref, w_ref, sems, w_sems):
    core, spot = info_ref[0], info_ref[1]
    near = pl.multiple_of(core * HALF, 16)
    far = pl.multiple_of((1 - core) * HALF, 16)
    copies = []
    for k, (half, other) in enumerate(((h0, o0), (h1, o1), (h2, o2), (h3, o3))):
        layer = lax.rem(spot + GROUP - k, GROUP)
        copies.append(pltpu.make_async_copy(half, w_ref.at[layer, pl.ds(near, HALF)], w_sems.at[2 * k]))
        copies.append(pltpu.make_async_copy(other, w_ref.at[layer, pl.ds(far, HALF)], w_sems.at[2 * k + 1]))
    for k, own in enumerate((own0, own1, own2, own3, term_own)):
        if k < GROUP:
            halo = GROUP - 1
            before, target, after = (gate_ref.at[lax.rem(spot + GROUP + n - k, GROUP)] for n in (-1, 0, 1))
        else:
            halo, before, target, after = STRIP, term_ref, term_ref, term_ref
        at = k * (GROUP - 1)
        moves = (
            (lasts.at[pl.ds(at, halo)], before, 0, halo, 0),
            (own, target, halo, STRIP, 0),
            (leads.at[pl.ds(at, halo)], after, halo + STRIP, halo, 0),
            (edge.at[pl.ds(20 + at, halo)], before, 0, halo, ROWS),
            (edge.at[pl.ds(k * STRIP, STRIP)], target, halo, STRIP, ROWS),
            (edge.at[pl.ds(36 + at, halo)], after, halo + STRIP, halo, ROWS),
        )
        for j, (a, place_ref, col, count, row) in enumerate(moves):
            b = place_ref.at[pl.ds(col, count), pl.ds(row, ROWS if row == 0 else 2 * PAD)]
            copies.append(pltpu.make_async_copy(a, b, sems.at[k, j]))
    for copy in copies:
        copy.start()
    for copy in copies:
        copy.wait()


def gate_call(info, gates, term, lasts, leads, edge, half, other):
    vmem = pl.BlockSpec(memory_space=pltpu.VMEM)
    hbm = pl.BlockSpec(memory_space=pl.ANY)
    return pl.pallas_call(
        gate_kernel,
        out_shape=(
            jax.ShapeDtypeStruct((GROUP, SEND, WIN, CH), BF),
            jax.ShapeDtypeStruct((3 * STRIP, WIN, CH), BF),
            jax.ShapeDtypeStruct((GROUP, TAPS, CH), BF),
        ),
        in_specs=[pl.BlockSpec(memory_space=pltpu.SMEM)] + [hbm] * 16,
        out_specs=(vmem,) * 3,
        scratch_shapes=[pltpu.SemaphoreType.DMA((GROUP + 1, 6)), pltpu.SemaphoreType.DMA((8,))],
        compiler_params=pltpu.CompilerParams(vmem_limit_bytes=TURN_VMEM),
        cost_estimate=pl.CostEstimate(flops=0, bytes_accessed=8 * 2**20, transcendentals=0),
    )(info, *gates, term, lasts, leads, edge, *half, *other)


TURN_CHUNKS = (5, 4, 3, 4)


def turn_kernel(first, *refs):
    (info_ref, term_ref), refs = refs[:2], refs[2:]
    if first:
        by_distance, (gate, w, out_ref, r, cur, xs) = refs[:4], refs[4:]
        for k in range(GROUP):
            r[lax.rem(info_ref[1] + GROUP - k, GROUP)] = by_distance[k][...]
    else:
        (mid_ref, left_ref, right_ref, rows_ref, r, gate, w, out_ref, cur, xs) = refs

    if first:
        cur[...] = term_ref[...].astype(F32)
    else:
        top = info_ref[2] == 1

        @pl.when(top)
        def _():
            cur[...] = term_ref[...].astype(F32)

        @pl.when(jnp.logical_not(top))
        def _():
            for i, ref in enumerate((left_ref, mid_ref, right_ref)):
                place(cur, i * STRIP, STRIP, ref[...], rows_ref[i * STRIP : (i + 1) * STRIP])

    for col in range(0, 3 * STRIP, 4):
        build(xs, 0, col, cur[col : col + 4], 4)

    for step in range(GROUP):
        layer = GROUP - 1 - step
        total = SEND - 2 * step
        size = TURN_CHUNKS[step]
        for col in range(0, total, size):
            change = conv(xs, step % 2, col, size, w, layer)
            open_ = gate[layer, step + col : step + col + size].reshape(size * WIN, CH) > 0
            x = r[layer, step + col : step + col + size].reshape(size * WIN, CH).astype(F32)
            x = x + (cur[1 + col : 1 + col + size].reshape(size * WIN, CH) + jnp.where(open_, 0.5 * change, 0.0))
            field = x.reshape(size, WIN, CH)
            cur[col : col + size] = field
            if step < GROUP - 1:
                build(xs, 1 - step % 2, col, field, size)
        inner = GROUP - 1 - step
        out_ref[layer] = cur[inner : inner + STRIP, 0:ROWS, :].astype(BF)


def turn_call(info, term, incoming, r, gate, w):
    first = incoming is None
    vmem = pl.BlockSpec(memory_space=pltpu.VMEM)
    pieces = (*r, gate, w) if first else (*incoming, r, gate, w)
    out = jax.ShapeDtypeStruct((GROUP, STRIP, ROWS, CH), BF)
    ordered = jax.ShapeDtypeStruct((GROUP, SEND, WIN, CH), BF)
    return pl.pallas_call(
        functools.partial(turn_kernel, first),
        out_shape=(out, ordered) if first else out,
        in_specs=[pl.BlockSpec(memory_space=pltpu.SMEM), vmem] + [vmem] * len(pieces),
        out_specs=(vmem, vmem) if first else vmem,
        scratch_shapes=[
            pltpu.VMEM((3 * STRIP, WIN, CH), F32),
            pltpu.VMEM((2, 3 * STRIP, WIN, 3 * CH), BF),
        ],
        compiler_params=pltpu.CompilerParams(vmem_limit_bytes=TURN_VMEM),
        cost_estimate=pl.CostEstimate(flops=2 * 2240 * TAPS * CH, bytes_accessed=8 * 2**20, transcendentals=0),
    )(info, term, *pieces)


def pack_kernel(info_ref, *refs):
    fields, out_ref = refs[:-1], refs[-1]
    row = lax.broadcasted_iota(jnp.int32, (1, 2 * PAD, CH), 1)
    before = (row >= PAD).astype(F32).astype(BF)
    after = (row < PAD).astype(F32).astype(BF)
    at = 0
    for ref in fields:
        count = ref.shape[0]

        @pl.when(info_ref[0] == 0)
        def _():
            out_ref[at : at + count] = ref[:, ROWS - 2 * PAD :, :] * before

        @pl.when(info_ref[0] == 1)
        def _():
            out_ref[at : at + count] = ref[:, : 2 * PAD, :] * after

        at += count


def pack(info, *fields):
    vmem = pl.BlockSpec(memory_space=pltpu.VMEM)
    count = sum(f.shape[0] for f in fields)
    return pl.pallas_call(
        pack_kernel,
        out_shape=jax.ShapeDtypeStruct((count, 2 * PAD, CH), BF),
        in_specs=[pl.BlockSpec(memory_space=pltpu.SMEM)] + [vmem] * len(fields),
        out_specs=vmem,
        compiler_params=pltpu.CompilerParams(vmem_limit_bytes=4 * 2**20),
        cost_estimate=pl.CostEstimate(flops=0, bytes_accessed=count * 2**14, transcendentals=0),
    )(info, *fields)


def on_device(states, weights, guess, terminal):
    groups = lax.axis_size("lx")
    zs = lax.axis_size("col")
    core = lax.axis_index("row")
    spot = lax.axis_index("ly")
    top = lax.axis_index("lx") == groups - 1
    info = jnp.stack([core, spot, top.astype(core.dtype)]).astype(jnp.int32)

    def in_group(value, shift):
        return lax.ppermute(value, "ly", [(y, (y + shift) % GROUP) for y in range(GROUP)])

    def z_up(value):
        return lax.ppermute(value, "col", [(i, i + 1) for i in range(zs - 1)])

    def z_down(value):
        return lax.ppermute(value, "col", [(i + 1, i) for i in range(zs - 1)])

    def core_swap(value):
        return lax.ppermute(value, "row", [(0, 1), (1, 0)])

    def to_other(*fields):
        return core_swap(pack(info, *fields))

    def turn(value):
        return jnp.swapaxes(value, -3, -2)

    own = turn(guess[0].astype(BF))
    above = lax.ppermute(own, ("lx", "ly"), [(d, d - 1) for d in range(1, groups * GROUP)])
    states, terminal, _ = lax.optimization_barrier((states, terminal, own))

    sources = [(states[3], 6), (states[2], 5), (states[1], 4), (states[0], 3)]
    lasts = z_up(turn(jnp.concatenate([f[:, COLS - h :] for f, h in sources], axis=1)))
    leads = z_down(turn(jnp.concatenate([f[:, :h] for f, h in sources], axis=1)))
    turned = turn(states)
    term = turn(terminal.astype(BF))

    def strip(field, target):
        return lax.dynamic_slice_in_dim(field, lax.rem(target, GROUP) * STRIP, STRIP, axis=0)

    gates = [strip(turned[0], spot)] + [in_group(strip(turned[0], spot + k), k) for k in range(1, GROUP)]
    flat = weights.reshape(DEPTH * TAPS, CH)
    half = lax.dynamic_slice(flat, (core * HALF, 0), (HALF, CH))
    rest = lax.dynamic_slice(flat, ((1 - core) * HALF, 0), (HALF, CH))
    halves = [half, in_group(half, 1)]
    edge = to_other(turned.reshape(DEPTH * COLS, ROWS, CH)).reshape(DEPTH, COLS, 2 * PAD, CH)
    above, lasts, leads, edge, term, half, rest, *gates = lax.optimization_barrier(
        (above, lasts, leads, edge, term, half, rest, *gates)
    )

    mid = jnp.where(jnp.logical_and(top, spot == GROUP - 1), term, above)
    left = z_up(mid[COLS - HALO :])
    right = z_down(mid[:HALO])
    tiles = GROUP * zs

    def beside(value, shift):
        pairs = []
        for tile in range(tiles):
            target = tile + shift
            if 0 <= target < tiles:
                pairs.append((tile % GROUP * zs + tile // GROUP, target % GROUP * zs + target // GROUP))
        return lax.ppermute(value, ("ly", "col"), pairs)

    term_strip = strip(term, spot)
    g_lasts = beside(jnp.concatenate([g[1:] for g in gates] + [term_strip], axis=0), 1)
    g_leads = beside(jnp.concatenate([g[:-1] for g in gates] + [term_strip], axis=0), -1)
    halves += [in_group(half, 2), in_group(half, 3)]
    outer = to_other(lasts, leads, left, mid, right)
    relaxed, *rs = fine_call(
        info, mid, left, right, outer[36:], turned, lasts, leads, edge, outer, flat.reshape(DEPTH, TAPS, CH)
    )

    g_lasts, g_leads, *halves, r0 = lax.optimization_barrier((g_lasts, g_leads, *halves, rs[0]))
    rs = [r0] + [in_group(rs[k], k) for k in range(1, GROUP)]
    others = [rest] + [core_swap(h) for h in halves[1:]]
    g_edge = to_other(*gates, term_strip, g_lasts, g_leads)
    gates, term_strip, group_weights = gate_call(info, gates, term_strip, g_lasts, g_leads, g_edge, halves, others)

    def across(value, shift):
        pairs = []
        for x in range(1, groups):
            for tile in range(tiles):
                target = tile + shift
                if 0 <= target < tiles:
                    start = (x * GROUP + tile % GROUP) * zs + tile // GROUP
                    end = ((x - 1) * GROUP + target % GROUP) * zs + target // GROUP
                    pairs.append((start, end))
        return lax.ppermute(value, ("lx", "ly", "col"), pairs)

    us, r = turn_call(info, term_strip, None, rs, gates, group_weights)
    for _ in range(groups - 1):
        low = us[0]
        u_left, u_right, u_mid = across(low, 1), across(low, -1), across(low, 0)
        u_rows = to_other(u_left, u_mid, u_right)
        us = turn_call(info, term_strip, (u_mid, u_left, u_right, u_rows), r, gates, group_weights)

    def of_interval(target):
        return lax.dynamic_index_in_dim(us, target, 0, keepdims=False)

    back = [of_interval(spot)] + [in_group(of_interval(lax.rem(spot + k, GROUP)), k) for k in range(1, GROUP)]
    stacked = jnp.stack(back)
    ordered = [
        lax.dynamic_index_in_dim(stacked, lax.rem(spot + GROUP - s, GROUP), 0, keepdims=False) for s in range(GROUP)
    ]
    corrected = turn(jnp.concatenate(ordered, axis=0).astype(F32))
    return (corrected[None], turn(relaxed))


def solution(mesh):
    shape = mesh.devices.shape
    split = Mesh(
        mesh.devices.reshape((shape[0] // GROUP, GROUP) + shape[1:]), ("lx", "ly") + tuple(mesh.axis_names[1:])
    )
    layer = ("lx", "ly")
    in_specs = (
        P(layer, "row", "col", None),
        P(layer, None, None, None, None),
        P(layer, "row", "col", None),
        P("row", "col", None),
    )
    out_specs = (P(layer, "row", "col", None), P(layer, "row", "col", None))
    return jax.shard_map(on_device, mesh=split, in_specs=in_specs, out_specs=out_specs, check_vma=False)
```

```python
import functools

import jax
import jax.experimental.pallas as pl
import jax.numpy as jnp
from jax import lax
from jax.experimental.pallas import tpu as pltpu
from jax.sharding import Mesh
from jax.sharding import PartitionSpec as P

BF = jnp.bfloat16
F32 = jnp.float32
CH = 256
ROWS = 64
PAD = 8
WIN = ROWS + 2 * PAD
COLS = 16
GROUP = 4
DEPTH = 4
STRIP = COLS // GROUP
SEND = STRIP + 2 * (GROUP - 1)
HALO = 7
WIDE = COLS + 2 * HALO
FINE_COLS = (28, 26, 24, 22)
HALF = 9 * CH // 2
CHUNK = 5
FINE_VMEM = 24 * 2**20
TURN_VMEM = 10 * 2**20
TAPS = 9 * CH


def build(xs, buf, col, x, count):
    field = x.reshape(count, WIN, CH)
    below = pltpu.roll(field, WIN - 1, 1)
    above = pltpu.roll(field, 1, 1)
    for tap, value in enumerate((below, field, above)):
        xs[buf, pl.ds(col, count), :, tap * CH : (tap + 1) * CH] = value.astype(BF)


def conv(xs, buf, col, count, w_ref, slot):
    total = None
    for b in range(3):
        for a in range(3):
            piece = xs[buf, pl.ds(col + 2 - b, count), :, a * CH : (a + 1) * CH].reshape(count * WIN, CH)
            tap = (a * 3 + b) * CH
            part = lax.dot_general(
                piece, w_ref[slot, tap : tap + CH, :], (((1,), (1,)), ((), ())), preferred_element_type=F32
            )
            total = part if total is None else total + part
    return total


def place(cur, col, count, piece, block):
    cur[col : col + count, 0:ROWS, :] = piece.astype(F32)
    cur[col : col + count, ROWS:WIN, :] = block.astype(F32)


def in_chunks(total, body):
    for col in range(0, total, CHUNK):
        body(col, min(CHUNK, total - col))


FIELDS = ((0, 6), (6, 5), (11, 4), (15, 3))
STARTS = (0, 28, 54, 78)


def fine_kernel(info_ref, mid_ref, left_ref, right_ref, rows_ref, own_hbm, lasts_hbm, leads_hbm, edge_hbm, outer_hbm, w,
                relaxed_ref, r0_ref, r1_ref, r2_ref, r3_ref, cur, xs, coarse, window, side, side_sem):
    side_copies = []
    for step in range(DEPTH):
        at, halo = FIELDS[step]
        start = STARTS[step]
        layer = DEPTH - 1 - step
        moves = (
            (lasts_hbm.at[pl.ds(at, halo)], side.at[pl.ds(start, halo), pl.ds(0, ROWS)]),
            (own_hbm.at[layer], side.at[pl.ds(start + halo, COLS), pl.ds(0, ROWS)]),
            (leads_hbm.at[pl.ds(at, halo)], side.at[pl.ds(start + halo + COLS, halo), pl.ds(0, ROWS)]),
            (outer_hbm.at[pl.ds(at, halo)], side.at[pl.ds(start, halo), pl.ds(ROWS, 2 * PAD)]),
            (edge_hbm.at[layer], side.at[pl.ds(start + halo, COLS), pl.ds(ROWS, 2 * PAD)]),
            (outer_hbm.at[pl.ds(18 + at, halo)], side.at[pl.ds(start + halo + COLS, halo), pl.ds(ROWS, 2 * PAD)]),
        )
        side_copies.append([pltpu.make_async_copy(a, b, side_sem.at[step, i]) for i, (a, b) in enumerate(moves)])
    for step in (3, 0, 1, 2):
        for copy in side_copies[step]:
            copy.start()
    spot = info_ref[1]
    place(cur, 0, HALO, left_ref[...], rows_ref[0:HALO])
    place(cur, HALO, COLS, mid_ref[...], rows_ref[HALO : HALO + COLS])
    place(cur, HALO + COLS, HALO, right_ref[...], rows_ref[HALO + COLS : WIDE])
    in_chunks(WIDE, lambda col, count: build(xs, 0, col, cur[col : col + count], count))

    def wait(step):
        for copy in side_copies[step]:
            copy.wait()

    wait(3)

    def coarse_chunk(col, count):
        gate = side[pl.ds(STARTS[3] + col, count)].reshape(count * WIN, CH) > 0
        change = conv(xs, 0, col + 3, count, w, 0)
        x = cur[pl.ds(col + 4, count)].reshape(count * WIN, CH) + jnp.where(gate, 0.5 * change, 0.0)
        coarse[pl.ds(col, count)] = x.reshape(count, WIN, CH)

    in_chunks(22, coarse_chunk)

    for step in range(DEPTH):
        layer = DEPTH - 1 - step
        if step < DEPTH - 1:
            wait(step)

        def chunk(col, count):
            gate = side[pl.ds(STARTS[step] + col, count)].reshape(count * WIN, CH) > 0
            change = conv(xs, step % 2, col, count, w, layer)
            x = cur[pl.ds(col + 1, count)].reshape(count * WIN, CH) + jnp.where(gate, 0.125 * change, 0.0)
            field = x.reshape(count, WIN, CH)
            cur[pl.ds(col, count)] = field
            if step < DEPTH - 1:
                build(xs, 1 - step % 2, col, field, count)
            else:
                window[pl.ds(col, count)] = (field - coarse[pl.ds(col, count)]).astype(BF)

        in_chunks(FINE_COLS[step], chunk)
        first = HALO - 1 - step
        relaxed_ref[layer] = cur[first : first + COLS, 0:ROWS, :].astype(BF)
    for k, ref in enumerate((r0_ref, r1_ref, r2_ref, r3_ref)):
        ref[...] = window[pl.ds(lax.rem(spot + k, GROUP) * STRIP, SEND)]


def fine_call(info, mid, left, right, rows, own, lasts, leads, edge, outer, w):
    vmem = pl.BlockSpec(memory_space=pltpu.VMEM)
    hbm = pl.BlockSpec(memory_space=pl.ANY)
    return pl.pallas_call(
        fine_kernel,
        out_shape=(jax.ShapeDtypeStruct((DEPTH, COLS, ROWS, CH), BF),)
        + (jax.ShapeDtypeStruct((SEND, WIN, CH), BF),) * GROUP,
        in_specs=[pl.BlockSpec(memory_space=pltpu.SMEM)] + [vmem] * 4 + [hbm] * 5 + [vmem],
        out_specs=(vmem,) * (1 + GROUP),
        scratch_shapes=[
            pltpu.VMEM((WIDE, WIN, CH), F32),
            pltpu.VMEM((2, WIDE, WIN, 3 * CH), BF),
            pltpu.VMEM((22, WIN, CH), F32),
            pltpu.VMEM((22, WIN, CH), BF),
            pltpu.VMEM((100, WIN, CH), BF),
            pltpu.SemaphoreType.DMA((DEPTH, 6)),
        ],
        compiler_params=pltpu.CompilerParams(vmem_limit_bytes=FINE_VMEM),
        cost_estimate=pl.CostEstimate(flops=2 * 9760 * TAPS * CH, bytes_accessed=14 * 2**20, transcendentals=0),
    )(info, mid, left, right, rows, own, lasts, leads, edge, outer, w)


def gate_kernel(info_ref, own0, own1, own2, own3, term_own, lasts, leads, edge, h0, h1, h2, h3, o0, o1, o2, o3,
                gate_ref, term_ref, w_ref, sems, w_sems):
    core, spot = info_ref[0], info_ref[1]
    near = pl.multiple_of(core * HALF, 16)
    far = pl.multiple_of((1 - core) * HALF, 16)
    copies = []
    for k, (half, other) in enumerate(((h0, o0), (h1, o1), (h2, o2), (h3, o3))):
        layer = lax.rem(spot + GROUP - k, GROUP)
        copies.append(pltpu.make_async_copy(half, w_ref.at[layer, pl.ds(near, HALF)], w_sems.at[2 * k]))
        copies.append(pltpu.make_async_copy(other, w_ref.at[layer, pl.ds(far, HALF)], w_sems.at[2 * k + 1]))
    for k, own in enumerate((own0, own1, own2, own3, term_own)):
        if k < GROUP:
            halo = GROUP - 1
            before, target, after = (gate_ref.at[lax.rem(spot + GROUP + n - k, GROUP)] for n in (-1, 0, 1))
        else:
            halo, before, target, after = STRIP, term_ref, term_ref, term_ref
        at = k * (GROUP - 1)
        moves = (
            (lasts.at[pl.ds(at, halo)], before, 0, halo, 0),
            (own, target, halo, STRIP, 0),
            (leads.at[pl.ds(at, halo)], after, halo + STRIP, halo, 0),
            (edge.at[pl.ds(20 + at, halo)], before, 0, halo, ROWS),
            (edge.at[pl.ds(k * STRIP, STRIP)], target, halo, STRIP, ROWS),
            (edge.at[pl.ds(36 + at, halo)], after, halo + STRIP, halo, ROWS),
        )
        for j, (a, place_ref, col, count, row) in enumerate(moves):
            b = place_ref.at[pl.ds(col, count), pl.ds(row, ROWS if row == 0 else 2 * PAD)]
            copies.append(pltpu.make_async_copy(a, b, sems.at[k, j]))
    for copy in copies:
        copy.start()
    for copy in copies:
        copy.wait()


def gate_call(info, gates, term, lasts, leads, edge, half, other):
    vmem = pl.BlockSpec(memory_space=pltpu.VMEM)
    hbm = pl.BlockSpec(memory_space=pl.ANY)
    return pl.pallas_call(
        gate_kernel,
        out_shape=(
            jax.ShapeDtypeStruct((GROUP, SEND, WIN, CH), BF),
            jax.ShapeDtypeStruct((3 * STRIP, WIN, CH), BF),
            jax.ShapeDtypeStruct((GROUP, TAPS, CH), BF),
        ),
        in_specs=[pl.BlockSpec(memory_space=pltpu.SMEM)] + [hbm] * 16,
        out_specs=(vmem,) * 3,
        scratch_shapes=[pltpu.SemaphoreType.DMA((GROUP + 1, 6)), pltpu.SemaphoreType.DMA((8,))],
        compiler_params=pltpu.CompilerParams(vmem_limit_bytes=TURN_VMEM),
        cost_estimate=pl.CostEstimate(flops=0, bytes_accessed=8 * 2**20, transcendentals=0),
    )(info, *gates, term, lasts, leads, edge, *half, *other)


TURN_CHUNKS = (5, 4, 3, 4)


def turn_kernel(first, *refs):
    (info_ref, term_ref), refs = refs[:2], refs[2:]
    if first:
        by_distance, (gate, w, out_ref, r, cur, xs) = refs[:4], refs[4:]
        for k in range(GROUP):
            r[lax.rem(info_ref[1] + GROUP - k, GROUP)] = by_distance[k][...]
    else:
        (mid_ref, left_ref, right_ref, rows_ref, r, gate, w, out_ref, cur, xs) = refs

    if first:
        cur[...] = term_ref[...].astype(F32)
    else:
        top = info_ref[2] == 1

        @pl.when(top)
        def _():
            cur[...] = term_ref[...].astype(F32)

        @pl.when(jnp.logical_not(top))
        def _():
            for i, ref in enumerate((left_ref, mid_ref, right_ref)):
                place(cur, i * STRIP, STRIP, ref[...], rows_ref[i * STRIP : (i + 1) * STRIP])

    for col in range(0, 3 * STRIP, 4):
        build(xs, 0, col, cur[col : col + 4], 4)

    for step in range(GROUP):
        layer = GROUP - 1 - step
        total = SEND - 2 * step
        size = TURN_CHUNKS[step]
        for col in range(0, total, size):
            change = conv(xs, step % 2, col, size, w, layer)
            open_ = gate[layer, step + col : step + col + size].reshape(size * WIN, CH) > 0
            x = r[layer, step + col : step + col + size].reshape(size * WIN, CH).astype(F32)
            x = x + (cur[1 + col : 1 + col + size].reshape(size * WIN, CH) + jnp.where(open_, 0.5 * change, 0.0))
            field = x.reshape(size, WIN, CH)
            cur[col : col + size] = field
            if step < GROUP - 1:
                build(xs, 1 - step % 2, col, field, size)
        inner = GROUP - 1 - step
        out_ref[layer] = cur[inner : inner + STRIP, 0:ROWS, :].astype(BF)


def turn_call(info, term, incoming, r, gate, w):
    first = incoming is None
    vmem = pl.BlockSpec(memory_space=pltpu.VMEM)
    pieces = (*r, gate, w) if first else (*incoming, r, gate, w)
    out = jax.ShapeDtypeStruct((GROUP, STRIP, ROWS, CH), BF)
    ordered = jax.ShapeDtypeStruct((GROUP, SEND, WIN, CH), BF)
    return pl.pallas_call(
        functools.partial(turn_kernel, first),
        out_shape=(out, ordered) if first else out,
        in_specs=[pl.BlockSpec(memory_space=pltpu.SMEM), vmem] + [vmem] * len(pieces),
        out_specs=(vmem, vmem) if first else vmem,
        scratch_shapes=[
            pltpu.VMEM((3 * STRIP, WIN, CH), F32),
            pltpu.VMEM((2, 3 * STRIP, WIN, 3 * CH), BF),
        ],
        compiler_params=pltpu.CompilerParams(vmem_limit_bytes=TURN_VMEM),
        cost_estimate=pl.CostEstimate(flops=2 * 2240 * TAPS * CH, bytes_accessed=8 * 2**20, transcendentals=0),
    )(info, term, *pieces)


def pack_kernel(info_ref, *refs):
    fields, out_ref = refs[:-1], refs[-1]
    row = lax.broadcasted_iota(jnp.int32, (1, 2 * PAD, CH), 1)
    before = (row >= PAD).astype(F32).astype(BF)
    after = (row < PAD).astype(F32).astype(BF)
    at = 0
    for ref in fields:
        count = ref.shape[0]

        @pl.when(info_ref[0] == 0)
        def _():
            out_ref[at : at + count] = ref[:, ROWS - 2 * PAD :, :] * before

        @pl.when(info_ref[0] == 1)
        def _():
            out_ref[at : at + count] = ref[:, : 2 * PAD, :] * after

        at += count


def pack(info, *fields):
    vmem = pl.BlockSpec(memory_space=pltpu.VMEM)
    count = sum(f.shape[0] for f in fields)
    return pl.pallas_call(
        pack_kernel,
        out_shape=jax.ShapeDtypeStruct((count, 2 * PAD, CH), BF),
        in_specs=[pl.BlockSpec(memory_space=pltpu.SMEM)] + [vmem] * len(fields),
        out_specs=vmem,
        compiler_params=pltpu.CompilerParams(vmem_limit_bytes=4 * 2**20),
        cost_estimate=pl.CostEstimate(flops=0, bytes_accessed=count * 2**14, transcendentals=0),
    )(info, *fields)


def on_device(states, weights, guess, terminal):
    groups = lax.axis_size("lx")
    layers = groups * GROUP
    zs = lax.axis_size("col")
    core = lax.axis_index("row")
    spot = lax.axis_index("ly")
    top = lax.axis_index("lx") == groups - 1
    info = jnp.stack([core, spot, top.astype(core.dtype)]).astype(jnp.int32)

    def in_group(value, shift):
        return lax.ppermute(value, "ly", [(y, (y + shift) % GROUP) for y in range(GROUP)])

    def z_up(value):
        return lax.ppermute(value, "col", [(i, i + 1) for i in range(zs - 1)])

    def z_down(value):
        return lax.ppermute(value, "col", [(i + 1, i) for i in range(zs - 1)])

    def core_swap(value):
        return lax.ppermute(value, "row", [(0, 1), (1, 0)])

    def to_other(*fields):
        return core_swap(pack(info, *fields))

    def turn(value):
        return jnp.swapaxes(value, -3, -2)

    own = turn(guess[0].astype(BF))
    above = lax.ppermute(own, ("lx", "ly"), [(d, (d - 1) % layers) for d in range(layers)])
    states, terminal, _ = lax.optimization_barrier((states, terminal, own))

    sources = [(states[3], 6), (states[2], 5), (states[1], 4), (states[0], 3)]
    lasts = z_up(turn(jnp.concatenate([f[:, COLS - h :] for f, h in sources], axis=1)))
    leads = z_down(turn(jnp.concatenate([f[:, :h] for f, h in sources], axis=1)))
    turned = turn(states)
    term = turn(terminal.astype(BF))

    def strip(field, target):
        return lax.dynamic_slice_in_dim(field, lax.rem(target, GROUP) * STRIP, STRIP, axis=0)

    gates = [strip(turned[0], spot)] + [in_group(strip(turned[0], spot + k), k) for k in range(1, GROUP)]
    flat = weights.reshape(DEPTH * TAPS, CH)
    half = lax.dynamic_slice(flat, (core * HALF, 0), (HALF, CH))
    rest = lax.dynamic_slice(flat, ((1 - core) * HALF, 0), (HALF, CH))
    halves = [half, in_group(half, 1)]
    edge = to_other(turned.reshape(DEPTH * COLS, ROWS, CH)).reshape(DEPTH, COLS, 2 * PAD, CH)
    above, lasts, leads, edge, term, half, rest, *gates = lax.optimization_barrier(
        (above, lasts, leads, edge, term, half, rest, *gates)
    )

    mid = jnp.where(jnp.logical_and(top, spot == GROUP - 1), term, above)
    left = z_up(mid[COLS - HALO :])
    right = z_down(mid[:HALO])
    tiles = GROUP * zs

    def beside(value, shift):
        pairs = []
        for tile in range(tiles):
            target = tile + shift
            if 0 <= target < tiles:
                pairs.append((tile % GROUP * zs + tile // GROUP, target % GROUP * zs + target // GROUP))
        return lax.ppermute(value, ("ly", "col"), pairs)

    term_strip = strip(term, spot)
    g_lasts = beside(jnp.concatenate([g[1:] for g in gates] + [term_strip], axis=0), 1)
    g_leads = beside(jnp.concatenate([g[:-1] for g in gates] + [term_strip], axis=0), -1)
    halves += [in_group(half, 2), in_group(half, 3)]
    outer = to_other(lasts, leads, left, mid, right)
    relaxed, *rs = fine_call(
        info, mid, left, right, outer[36:], turned, lasts, leads, edge, outer, flat.reshape(DEPTH, TAPS, CH)
    )

    g_lasts, g_leads, *halves, r0 = lax.optimization_barrier((g_lasts, g_leads, *halves, rs[0]))
    rs = [r0] + [in_group(rs[k], k) for k in range(1, GROUP)]
    others = [rest] + [core_swap(h) for h in halves[1:]]
    g_edge = to_other(*gates, term_strip, g_lasts, g_leads)
    gates, term_strip, group_weights = gate_call(info, gates, term_strip, g_lasts, g_leads, g_edge, halves, others)

    tile_here = lax.axis_index("col") * GROUP + spot

    def across(value, shift):
        pairs = []
        for x in range(groups):
            for tile in range(tiles):
                target = (tile + shift) % tiles
                start = (x * GROUP + tile % GROUP) * zs + tile // GROUP
                end = ((x - 1) % groups * GROUP + target % GROUP) * zs + target // GROUP
                pairs.append((start, end))
        moved = lax.ppermute(value, ("lx", "ly", "col"), pairs)
        if shift == 0:
            return moved
        return jnp.where(tile_here == (0 if shift > 0 else tiles - 1), jnp.zeros_like(moved), moved)

    us, r = turn_call(info, term_strip, None, rs, gates, group_weights)
    for _ in range(groups - 1):
        low = us[0]
        u_left, u_right, u_mid = across(low, 1), across(low, -1), across(low, 0)
        u_rows = to_other(u_left, u_mid, u_right)
        us = turn_call(info, term_strip, (u_mid, u_left, u_right, u_rows), r, gates, group_weights)

    def of_interval(target):
        return lax.dynamic_index_in_dim(us, target, 0, keepdims=False)

    back = [of_interval(spot)] + [in_group(of_interval(lax.rem(spot + k, GROUP)), k) for k in range(1, GROUP)]
    stacked = jnp.stack(back)
    ordered = [
        lax.dynamic_index_in_dim(stacked, lax.rem(spot + GROUP - s, GROUP), 0, keepdims=False) for s in range(GROUP)
    ]
    corrected = turn(jnp.concatenate(ordered, axis=0).astype(F32))
    return (corrected[None], turn(relaxed))


def solution(mesh):
    shape = mesh.devices.shape
    split = Mesh(
        mesh.devices.reshape((shape[0] // GROUP, GROUP) + shape[1:]), ("lx", "ly") + tuple(mesh.axis_names[1:])
    )
    layer = ("lx", "ly")
    in_specs = (
        P(layer, "row", "col", None),
        P(layer, None, None, None, None),
        P(layer, "row", "col", None),
        P("row", "col", None),
    )
    out_specs = (P(layer, "row", "col", None), P(layer, "row", "col", None))
    return jax.shard_map(on_device, mesh=split, in_specs=in_specs, out_specs=out_specs, check_vma=False)
```

```python
import functools

import jax
import jax.experimental.pallas as pl
import jax.numpy as jnp
from jax import lax
from jax.experimental.pallas import tpu as pltpu
from jax.sharding import Mesh
from jax.sharding import PartitionSpec as P

BF = jnp.bfloat16
F32 = jnp.float32
CH = 256
ROWS = 64
PAD = 8
WIN = ROWS + 2 * PAD
COLS = 16
GROUP = 4
DEPTH = 4
STRIP = COLS // GROUP
SEND = STRIP + 2 * (GROUP - 1)
HALO = 7
WIDE = COLS + 2 * HALO
FINE_COLS = (28, 26, 24, 22)
HALF = 9 * CH // 2
CHUNK = 5
FINE_VMEM = 24 * 2**20
TURN_VMEM = 10 * 2**20
TAPS = 9 * CH


def build(xs, buf, col, x, count):
    field = x.reshape(count, WIN, CH)
    below = pltpu.roll(field, WIN - 1, 1)
    above = pltpu.roll(field, 1, 1)
    for tap, value in enumerate((below, field, above)):
        xs[buf, pl.ds(col, count), :, tap * CH : (tap + 1) * CH] = value.astype(BF)


def conv(xs, buf, col, count, w_ref, slot):
    total = None
    for b in range(3):
        for a in range(3):
            piece = xs[buf, pl.ds(col + 2 - b, count), :, a * CH : (a + 1) * CH].reshape(count * WIN, CH)
            tap = (a * 3 + b) * CH
            part = lax.dot_general(
                piece, w_ref[slot, tap : tap + CH, :], (((1,), (1,)), ((), ())), preferred_element_type=F32
            )
            total = part if total is None else total + part
    return total


def place(cur, col, count, piece, block):
    cur[col : col + count, 0:ROWS, :] = piece.astype(F32)
    cur[col : col + count, ROWS:WIN, :] = block.astype(F32)


def in_chunks(total, body):
    for col in range(0, total, CHUNK):
        body(col, min(CHUNK, total - col))


FIELDS = ((0, 6), (6, 5), (11, 4), (15, 3))
STARTS = (0, 28, 54, 78)


def fine_kernel(info_ref, mid_ref, left_ref, right_ref, rows_ref, own_hbm, lasts_hbm, leads_hbm, edge_hbm, outer_hbm, w,
                relaxed_ref, r0_ref, r1_ref, r2_ref, r3_ref, cur, xs, coarse, window, side, side_sem):
    side_copies = []
    for step in range(DEPTH):
        at, halo = FIELDS[step]
        start = STARTS[step]
        layer = DEPTH - 1 - step
        moves = (
            (lasts_hbm.at[pl.ds(at, halo)], side.at[pl.ds(start, halo), pl.ds(0, ROWS)]),
            (own_hbm.at[layer], side.at[pl.ds(start + halo, COLS), pl.ds(0, ROWS)]),
            (leads_hbm.at[pl.ds(at, halo)], side.at[pl.ds(start + halo + COLS, halo), pl.ds(0, ROWS)]),
            (outer_hbm.at[pl.ds(at, halo)], side.at[pl.ds(start, halo), pl.ds(ROWS, 2 * PAD)]),
            (edge_hbm.at[layer], side.at[pl.ds(start + halo, COLS), pl.ds(ROWS, 2 * PAD)]),
            (outer_hbm.at[pl.ds(18 + at, halo)], side.at[pl.ds(start + halo + COLS, halo), pl.ds(ROWS, 2 * PAD)]),
        )
        side_copies.append([pltpu.make_async_copy(a, b, side_sem.at[step, i]) for i, (a, b) in enumerate(moves)])
    for step in (3, 0, 1, 2):
        for copy in side_copies[step]:
            copy.start()
    spot = info_ref[1]
    place(cur, 0, HALO, left_ref[...], rows_ref[0:HALO])
    place(cur, HALO, COLS, mid_ref[...], rows_ref[HALO : HALO + COLS])
    place(cur, HALO + COLS, HALO, right_ref[...], rows_ref[HALO + COLS : WIDE])
    in_chunks(WIDE, lambda col, count: build(xs, 0, col, cur[col : col + count], count))

    def wait(step):
        for copy in side_copies[step]:
            copy.wait()

    wait(3)

    def coarse_chunk(col, count):
        gate = side[pl.ds(STARTS[3] + col, count)].reshape(count * WIN, CH) > 0
        change = conv(xs, 0, col + 3, count, w, 0)
        x = cur[pl.ds(col + 4, count)].reshape(count * WIN, CH) + jnp.where(gate, 0.5 * change, 0.0)
        coarse[pl.ds(col, count)] = x.reshape(count, WIN, CH)

    in_chunks(22, coarse_chunk)

    for step in range(DEPTH):
        layer = DEPTH - 1 - step
        if step < DEPTH - 1:
            wait(step)

        def chunk(col, count):
            gate = side[pl.ds(STARTS[step] + col, count)].reshape(count * WIN, CH) > 0
            change = conv(xs, step % 2, col, count, w, layer)
            x = cur[pl.ds(col + 1, count)].reshape(count * WIN, CH) + jnp.where(gate, 0.125 * change, 0.0)
            field = x.reshape(count, WIN, CH)
            cur[pl.ds(col, count)] = field
            if step < DEPTH - 1:
                build(xs, 1 - step % 2, col, field, count)
            else:
                window[pl.ds(col, count)] = (field - coarse[pl.ds(col, count)]).astype(BF)

        in_chunks(FINE_COLS[step], chunk)
        first = HALO - 1 - step
        relaxed_ref[layer] = cur[first : first + COLS, 0:ROWS, :].astype(BF)
    for k, ref in enumerate((r0_ref, r1_ref, r2_ref, r3_ref)):
        ref[...] = window[pl.ds(lax.rem(spot + k, GROUP) * STRIP, SEND)]


def fine_call(info, mid, left, right, rows, own, lasts, leads, edge, outer, w):
    vmem = pl.BlockSpec(memory_space=pltpu.VMEM)
    hbm = pl.BlockSpec(memory_space=pl.ANY)
    return pl.pallas_call(
        fine_kernel,
        out_shape=(jax.ShapeDtypeStruct((DEPTH, COLS, ROWS, CH), BF),)
        + (jax.ShapeDtypeStruct((SEND, WIN, CH), BF),) * GROUP,
        in_specs=[pl.BlockSpec(memory_space=pltpu.SMEM)] + [vmem] * 4 + [hbm] * 5 + [vmem],
        out_specs=(vmem,) * (1 + GROUP),
        scratch_shapes=[
            pltpu.VMEM((WIDE, WIN, CH), F32),
            pltpu.VMEM((2, WIDE, WIN, 3 * CH), BF),
            pltpu.VMEM((22, WIN, CH), F32),
            pltpu.VMEM((22, WIN, CH), BF),
            pltpu.VMEM((100, WIN, CH), BF),
            pltpu.SemaphoreType.DMA((DEPTH, 6)),
        ],
        compiler_params=pltpu.CompilerParams(vmem_limit_bytes=FINE_VMEM),
        cost_estimate=pl.CostEstimate(flops=2 * 9760 * TAPS * CH, bytes_accessed=14 * 2**20, transcendentals=0),
    )(info, mid, left, right, rows, own, lasts, leads, edge, outer, w)


def gate_kernel(info_ref, own0, own1, own2, own3, term_own, lasts, leads, edge, h0, h1, h2, h3, o0, o1, o2, o3,
                gate_ref, term_ref, w_ref, sems, w_sems):
    core, spot = info_ref[0], info_ref[1]
    near = pl.multiple_of(core * HALF, 16)
    far = pl.multiple_of((1 - core) * HALF, 16)
    copies = []
    for k, (half, other) in enumerate(((h0, o0), (h1, o1), (h2, o2), (h3, o3))):
        layer = lax.rem(spot + GROUP - k, GROUP)
        copies.append(pltpu.make_async_copy(half, w_ref.at[layer, pl.ds(near, HALF)], w_sems.at[2 * k]))
        copies.append(pltpu.make_async_copy(other, w_ref.at[layer, pl.ds(far, HALF)], w_sems.at[2 * k + 1]))
    for k, own in enumerate((own0, own1, own2, own3, term_own)):
        if k < GROUP:
            halo = GROUP - 1
            before, target, after = (gate_ref.at[lax.rem(spot + GROUP + n - k, GROUP)] for n in (-1, 0, 1))
        else:
            halo, before, target, after = STRIP, term_ref, term_ref, term_ref
        at = k * (GROUP - 1)
        moves = (
            (lasts.at[pl.ds(at, halo)], before, 0, halo, 0),
            (own, target, halo, STRIP, 0),
            (leads.at[pl.ds(at, halo)], after, halo + STRIP, halo, 0),
            (edge.at[pl.ds(20 + at, halo)], before, 0, halo, ROWS),
            (edge.at[pl.ds(k * STRIP, STRIP)], target, halo, STRIP, ROWS),
            (edge.at[pl.ds(36 + at, halo)], after, halo + STRIP, halo, ROWS),
        )
        for j, (a, place_ref, col, count, row) in enumerate(moves):
            b = place_ref.at[pl.ds(col, count), pl.ds(row, ROWS if row == 0 else 2 * PAD)]
            copies.append(pltpu.make_async_copy(a, b, sems.at[k, j]))
    for copy in copies:
        copy.start()
    for copy in copies:
        copy.wait()


def gate_call(info, gates, term, lasts, leads, edge, half, other):
    vmem = pl.BlockSpec(memory_space=pltpu.VMEM)
    hbm = pl.BlockSpec(memory_space=pl.ANY)
    return pl.pallas_call(
        gate_kernel,
        out_shape=(
            jax.ShapeDtypeStruct((GROUP, SEND, WIN, CH), BF),
            jax.ShapeDtypeStruct((3 * STRIP, WIN, CH), BF),
            jax.ShapeDtypeStruct((GROUP, TAPS, CH), BF),
        ),
        in_specs=[pl.BlockSpec(memory_space=pltpu.SMEM)] + [hbm] * 16,
        out_specs=(vmem,) * 3,
        scratch_shapes=[pltpu.SemaphoreType.DMA((GROUP + 1, 6)), pltpu.SemaphoreType.DMA((8,))],
        compiler_params=pltpu.CompilerParams(vmem_limit_bytes=TURN_VMEM),
        cost_estimate=pl.CostEstimate(flops=0, bytes_accessed=8 * 2**20, transcendentals=0),
    )(info, *gates, term, lasts, leads, edge, *half, *other)


TURN_CHUNKS = (5, 4, 3, 4)


def turn_kernel(first, *refs):
    (info_ref, term_ref), refs = refs[:2], refs[2:]
    if first:
        by_distance, (gate, w, out_ref, r, cur, xs) = refs[:4], refs[4:]
        for k in range(GROUP):
            r[lax.rem(info_ref[1] + GROUP - k, GROUP)] = by_distance[k][...]
    else:
        (mid_ref, left_ref, right_ref, rows_ref, r, gate, w, out_ref, cur, xs) = refs

    if first:
        cur[...] = term_ref[...].astype(F32)
    else:
        top = info_ref[2] == 1

        @pl.when(top)
        def _():
            cur[...] = term_ref[...].astype(F32)

        @pl.when(jnp.logical_not(top))
        def _():
            for i, ref in enumerate((left_ref, mid_ref, right_ref)):
                place(cur, i * STRIP, STRIP, ref[...], rows_ref[i * STRIP : (i + 1) * STRIP])
            for i in (0, 2):
                keep = info_ref[3 + i // 2].astype(F32)
                cur[i * STRIP : (i + 1) * STRIP] = cur[i * STRIP : (i + 1) * STRIP] * keep

    for col in range(0, 3 * STRIP, 4):
        build(xs, 0, col, cur[col : col + 4], 4)

    for step in range(GROUP):
        layer = GROUP - 1 - step
        total = SEND - 2 * step
        size = TURN_CHUNKS[step]
        for col in range(0, total, size):
            change = conv(xs, step % 2, col, size, w, layer)
            open_ = gate[layer, step + col : step + col + size].reshape(size * WIN, CH) > 0
            x = r[layer, step + col : step + col + size].reshape(size * WIN, CH).astype(F32)
            x = x + (cur[1 + col : 1 + col + size].reshape(size * WIN, CH) + jnp.where(open_, 0.5 * change, 0.0))
            field = x.reshape(size, WIN, CH)
            cur[col : col + size] = field
            if step < GROUP - 1:
                build(xs, 1 - step % 2, col, field, size)
        inner = GROUP - 1 - step
        out_ref[layer] = cur[inner : inner + STRIP, 0:ROWS, :].astype(BF)


def turn_call(info, term, incoming, r, gate, w):
    first = incoming is None
    vmem = pl.BlockSpec(memory_space=pltpu.VMEM)
    pieces = (*r, gate, w) if first else (*incoming, r, gate, w)
    out = jax.ShapeDtypeStruct((GROUP, STRIP, ROWS, CH), BF)
    ordered = jax.ShapeDtypeStruct((GROUP, SEND, WIN, CH), BF)
    return pl.pallas_call(
        functools.partial(turn_kernel, first),
        out_shape=(out, ordered) if first else out,
        in_specs=[pl.BlockSpec(memory_space=pltpu.SMEM), vmem] + [vmem] * len(pieces),
        out_specs=(vmem, vmem) if first else vmem,
        scratch_shapes=[
            pltpu.VMEM((3 * STRIP, WIN, CH), F32),
            pltpu.VMEM((2, 3 * STRIP, WIN, 3 * CH), BF),
        ],
        compiler_params=pltpu.CompilerParams(vmem_limit_bytes=TURN_VMEM),
        cost_estimate=pl.CostEstimate(flops=2 * 2240 * TAPS * CH, bytes_accessed=8 * 2**20, transcendentals=0),
    )(info, term, *pieces)


def pack_kernel(info_ref, *refs):
    fields, out_ref = refs[:-1], refs[-1]
    row = lax.broadcasted_iota(jnp.int32, (1, 2 * PAD, CH), 1)
    before = (row >= PAD).astype(F32).astype(BF)
    after = (row < PAD).astype(F32).astype(BF)
    at = 0
    for ref in fields:
        count = ref.shape[0]

        @pl.when(info_ref[0] == 0)
        def _():
            out_ref[at : at + count] = ref[:, ROWS - 2 * PAD :, :] * before

        @pl.when(info_ref[0] == 1)
        def _():
            out_ref[at : at + count] = ref[:, : 2 * PAD, :] * after

        at += count


def pack(info, *fields):
    vmem = pl.BlockSpec(memory_space=pltpu.VMEM)
    count = sum(f.shape[0] for f in fields)
    return pl.pallas_call(
        pack_kernel,
        out_shape=jax.ShapeDtypeStruct((count, 2 * PAD, CH), BF),
        in_specs=[pl.BlockSpec(memory_space=pltpu.SMEM)] + [vmem] * len(fields),
        out_specs=vmem,
        compiler_params=pltpu.CompilerParams(vmem_limit_bytes=4 * 2**20),
        cost_estimate=pl.CostEstimate(flops=0, bytes_accessed=count * 2**14, transcendentals=0),
    )(info, *fields)


def on_device(states, weights, guess, terminal):
    groups = lax.axis_size("lx")
    zs = lax.axis_size("col")
    core = lax.axis_index("row")
    spot = lax.axis_index("ly")
    top = lax.axis_index("lx") == groups - 1
    tile_here = lax.axis_index("col") * GROUP + spot
    inner = [(tile_here != end).astype(core.dtype) for end in (0, zs * GROUP - 1)]
    info = jnp.stack([core, spot, top.astype(core.dtype)] + inner).astype(jnp.int32)

    def in_group(value, shift):
        return lax.ppermute(value, "ly", [(y, (y + shift) % GROUP) for y in range(GROUP)])

    def z_up(value):
        return lax.ppermute(value, "col", [(i, i + 1) for i in range(zs - 1)])

    def z_down(value):
        return lax.ppermute(value, "col", [(i + 1, i) for i in range(zs - 1)])

    def core_swap(value):
        return lax.ppermute(value, "row", [(0, 1), (1, 0)])

    def to_other(*fields):
        return core_swap(pack(info, *fields))

    def turn(value):
        return jnp.swapaxes(value, -3, -2)

    own = turn(guess[0].astype(BF))
    above = lax.ppermute(own, ("lx", "ly"), [(d, d - 1) for d in range(1, groups * GROUP)])
    states, terminal, _ = lax.optimization_barrier((states, terminal, own))

    sources = [(states[3], 6), (states[2], 5), (states[1], 4), (states[0], 3)]
    lasts = z_up(turn(jnp.concatenate([f[:, COLS - h :] for f, h in sources], axis=1)))
    leads = z_down(turn(jnp.concatenate([f[:, :h] for f, h in sources], axis=1)))
    turned = turn(states)
    term = turn(terminal.astype(BF))

    def strip(field, target):
        return lax.dynamic_slice_in_dim(field, lax.rem(target, GROUP) * STRIP, STRIP, axis=0)

    gates = [strip(turned[0], spot)] + [in_group(strip(turned[0], spot + k), k) for k in range(1, GROUP)]
    flat = weights.reshape(DEPTH * TAPS, CH)
    half = lax.dynamic_slice(flat, (core * HALF, 0), (HALF, CH))
    rest = lax.dynamic_slice(flat, ((1 - core) * HALF, 0), (HALF, CH))
    halves = [half, in_group(half, 1)]
    edge = to_other(turned.reshape(DEPTH * COLS, ROWS, CH)).reshape(DEPTH, COLS, 2 * PAD, CH)
    above, lasts, leads, edge, term, half, rest, *gates = lax.optimization_barrier(
        (above, lasts, leads, edge, term, half, rest, *gates)
    )

    mid = jnp.where(jnp.logical_and(top, spot == GROUP - 1), term, above)
    left = z_up(mid[COLS - HALO :])
    right = z_down(mid[:HALO])
    tiles = GROUP * zs

    def beside(value, shift):
        pairs = []
        for tile in range(tiles):
            target = tile + shift
            if 0 <= target < tiles:
                pairs.append((tile % GROUP * zs + tile // GROUP, target % GROUP * zs + target // GROUP))
        return lax.ppermute(value, ("ly", "col"), pairs)

    term_strip = strip(term, spot)
    g_lasts = beside(jnp.concatenate([g[1:] for g in gates] + [term_strip], axis=0), 1)
    g_leads = beside(jnp.concatenate([g[:-1] for g in gates] + [term_strip], axis=0), -1)
    halves += [in_group(half, 2), in_group(half, 3)]
    outer = to_other(lasts, leads, left, mid, right)
    relaxed, *rs = fine_call(
        info, mid, left, right, outer[36:], turned, lasts, leads, edge, outer, flat.reshape(DEPTH, TAPS, CH)
    )

    g_lasts, g_leads, *halves, r0 = lax.optimization_barrier((g_lasts, g_leads, *halves, rs[0]))
    rs = [r0] + [in_group(rs[k], k) for k in range(1, GROUP)]
    others = [rest] + [core_swap(h) for h in halves[1:]]
    g_edge = to_other(*gates, term_strip, g_lasts, g_leads)
    gates, term_strip, group_weights = gate_call(info, gates, term_strip, g_lasts, g_leads, g_edge, halves, others)

    def across(value, shift):
        pairs = []
        for x in range(groups):
            for tile in range(tiles):
                target = (tile + shift) % tiles
                start = (x * GROUP + tile % GROUP) * zs + tile // GROUP
                end = ((x - 1) % groups * GROUP + target % GROUP) * zs + target // GROUP
                pairs.append((start, end))
        return lax.ppermute(value, ("lx", "ly", "col"), pairs)

    us, r = turn_call(info, term_strip, None, rs, gates, group_weights)
    for _ in range(groups - 1):
        low = us[0]
        u_left, u_right, u_mid = across(low, 1), across(low, -1), across(low, 0)
        u_rows = to_other(u_left, u_mid, u_right)
        us = turn_call(info, term_strip, (u_mid, u_left, u_right, u_rows), r, gates, group_weights)

    def of_interval(target):
        return lax.dynamic_index_in_dim(us, target, 0, keepdims=False)

    back = [of_interval(spot)] + [in_group(of_interval(lax.rem(spot + k, GROUP)), k) for k in range(1, GROUP)]
    stacked = jnp.stack(back)
    ordered = [
        lax.dynamic_index_in_dim(stacked, lax.rem(spot + GROUP - s, GROUP), 0, keepdims=False) for s in range(GROUP)
    ]
    corrected = turn(jnp.concatenate(ordered, axis=0).astype(F32))
    return (corrected[None], turn(relaxed))


def solution(mesh):
    shape = mesh.devices.shape
    split = Mesh(
        mesh.devices.reshape((shape[0] // GROUP, GROUP) + shape[1:]), ("lx", "ly") + tuple(mesh.axis_names[1:])
    )
    layer = ("lx", "ly")
    in_specs = (
        P(layer, "row", "col", None),
        P(layer, None, None, None, None),
        P(layer, "row", "col", None),
        P("row", "col", None),
    )
    out_specs = (P(layer, "row", "col", None), P(layer, "row", "col", None))
    return jax.shard_map(on_device, mesh=split, in_specs=in_specs, out_specs=out_specs, check_vma=False)
```
